32 devices in a mesh: node: 16 (over z, x, core), feat: 2 (over y).
Axes of the slice: x: 2, y: 2, z: 4, core: 2. Of those that a mesh axis runs over, the one named last changes fastest.
Arguments:
- covariates: bfloat16 [256, 65536], P('feat', 'node'), may hold values from 0 to 0.9921875
- pseudo: bfloat16 [16, 65536], P(None, 'node'), may hold values from -6 to 6
- honest: int32 [65536], P('node'), may hold values 0 or 1
- destination: int32 [65536, 1], P('node'), may hold values from 0 to 31; in each aligned block of 4096 rows (0 to 4095, 4096 to 8191, ...) at most 256 rows name the same one
- node_slot: int32 [32], replicated, may hold values from 0 to 31, each once
Outputs:
- histogram: float32 [32, 256, 17, 256], P('node', 'feat')
- best_gain: float32 [32], P('node')
The draws below stay inside these ranges and needn't reach their ends.
Inputs may be any that keep to these rules, and one draw needn't show every extreme that they name: `destination`: in the rows of one device no child node is named by more than 256 rows. Each slot appears once; child node n belongs to the owner node_slot[n] // 2 along node.
All inputs are finite; a program needn't handle non-finite values. No bound on the sum of `honest` on one device may be relied on, other than what follows from the above.
Results may differ from the reference program's by a relative error of at most 0.0003.
Values may be sent and summed in bfloat16 or wider, within the bound.
A program may use at most 64 MiB of HBM per device.

```python
import math
import jax
import jax.numpy as jnp
import numpy as np
from jax import lax

F = 256
B = 256
PSEUDO = 16
ROWS_DEV = 4096
ROWS = 65536
NODES = 32
MOST = 256


def with_ends(drawn, rng, low, largest):
    place = [jax.random.randint(jax.random.fold_in(rng, axis), (), 0, length) for axis, length in enumerate(drawn.shape)]
    longest = drawn.shape.index(max(drawn.shape))
    neighbour = place[:longest] + [(place[longest] + 1) % drawn.shape[longest]] + place[longest + 1:]
    return drawn.at[tuple(place)].set(low).at[tuple(neighbour)].set(largest)


def level_of(key, shape, shards, least, top_value):
    loudness = 1.0
    for dim, shards_of in shards:
        steps = jax.random.uniform(jax.random.fold_in(jax.random.fold_in(key, 6), dim), (shards_of,), jnp.float32, least / len(shards), top_value / len(shards))
        loudness = loudness * jnp.repeat(jnp.exp(steps), shape[dim] // shards_of).reshape((-1,) + (1,) * (len(shape) - 1 - dim))
    return loudness


def shared_out(own_key, own, number, rows, number_of, top, bound, skew):
    order = jax.random.permutation(own_key, number_of)
    heavy_load, common = shares(number_of, rows * top, bound, skew, True), shares(number_of, rows * top, bound, skew, False)
    places = jnp.arange(number_of)

    def named(sizes, turn):
        used = int((sizes > 0).sum())
        fixed = max(1, used // 4)
        moved = fixed + (places - fixed + turn * (used - fixed)) % max(1, number_of - fixed)
        return jnp.zeros((number_of,), jnp.int32).at[order[jnp.where(places < fixed, places, moved)]].set(jnp.asarray(sizes, jnp.int32))

    sizes = jnp.where(number % 4 == 0, named(heavy_load, number // 4), named(common, number - number // 4 - 1))
    mixed = jax.random.permutation(jax.random.fold_in(own, 3), number_of)
    source_of, receiver = mixed[0:number_of // 2 * 2:2], mixed[1:number_of // 2 * 2:2]
    slack = jnp.minimum(sizes[source_of] - 1, bound - sizes[receiver]) // 2
    slack = jnp.where((source_of == order[0]) | (receiver == order[0]) | (sizes[receiver] == 0), 0, jnp.maximum(slack, 0))
    moved = jax.random.randint(jax.random.fold_in(own, 4), (number_of // 2,), 0, 1 << 20) % (slack + 1)
    sizes = sizes.at[source_of].add(-moved).at[receiver].add(moved)
    labels = jnp.searchsorted(jnp.cumsum(sizes), jnp.arange(rows * top), side="right").astype(jnp.int32)
    listing = labels.reshape(top, rows).T
    listing = listing[jax.random.permutation(jax.random.fold_in(own, 1), rows)]
    turn = jax.random.randint(jax.random.fold_in(own, 2), (rows, 1), 0, top)
    return jnp.take_along_axis(listing, (jnp.arange(top)[None, :] + turn) % top, axis=1)


def shares(count, total, reach, lean, full):
    weights = [(1 << 20) // math.isqrt(grade ** lean) + 1 for grade in range(1, count + 1)]
    largest = reach if full else min(reach, max(-(-total // count), total * weights[0] // sum(weights)))
    least = 1 if total - largest >= count - 1 else 0
    given, rest = [largest] + [least] * (count - 1), total - largest - least * (count - 1)
    while rest > 0:
        movable = [i for i in range(1, count) if given[i] < largest] or [i for i in range(1, count) if given[i] < reach]
        mass, budget = sum([weights[i] for i in movable]), rest
        for i in movable:
            extra = min(reach - given[i], max(1, budget * weights[i] // mass), rest)
            given[i] = given[i] + extra
            rest = rest - extra
    return np.array(given)


def bell_draw(stream_key, shape, width, bound, pieces=(), dtype=jnp.bfloat16):
    values = width * jax.random.normal(stream_key, shape, jnp.float32)
    if pieces:
        values = values * level_of(stream_key, shape, pieces, -0.22, 0.18)
    return jnp.clip(values, -bound, bound).astype(dtype)


def setup_inputs(seed: int = 0) -> dict:
    keys = jax.random.split(jax.random.key(seed), 6)
    covariates = jnp.clip(0.9921875 * jax.random.uniform(keys[0], (F, ROWS), jnp.float32) ** level_of(keys[0], (F, ROWS), ((0, 2), (1, 16)), -0.2, 0.2), 0.0, 0.9921875).astype(jnp.bfloat16)
    pseudo = bell_draw(keys[1], (PSEUDO, ROWS), 1.0, 6.0, ((1, 16),))
    honest = with_ends((jax.random.randint(keys[2], (ROWS,), 0, 2) < 1).astype(jnp.int32), jax.random.fold_in(keys[2], 1), 0, 1)
    destination_keys = jax.random.split(jax.random.fold_in(keys[3], 1), ROWS // ROWS_DEV)
    destination_turns = jax.random.permutation(jax.random.fold_in(keys[3], 3), ROWS // ROWS_DEV)
    destination = jax.vmap(lambda own, number: shared_out(jax.random.fold_in(keys[3], 2), own, number, ROWS_DEV, NODES, 1, MOST, 2))(destination_keys, destination_turns).reshape((ROWS, 1))
    node_slot = jax.random.permutation(keys[4], NODES).astype(jnp.int32)
    return {"covariates": covariates, "pseudo": pseudo, "honest": honest, "destination": destination, "node_slot": node_slot}


def reference(covariates, pseudo, honest, destination, node_slot):
    bins = jnp.floor(covariates.astype(jnp.float32) * B).astype(jnp.int32)
    weight = (1 - honest).astype(jnp.float32)
    statistics = jnp.concatenate([weight[None, :], weight[None, :] * pseudo.astype(jnp.float32)], axis=0)
    target = node_slot[destination[:, 0]].astype(jnp.int32)
    stat_rows = jnp.transpose(statistics)

    def per_feature(bin_row):
        segment = target * B + bin_row
        return jax.ops.segment_sum(stat_rows, segment, num_segments=NODES * B)

    stacked = lax.map(per_feature, bins)
    histogram = jnp.transpose(stacked.reshape(F, NODES, B, PSEUDO + 1), (1, 0, 3, 2))
    left = jnp.cumsum(histogram, axis=3)
    total = left[:, :, :, -1:]
    right = total - left
    left_part = jnp.sum(left[:, :, 1:] * left[:, :, 1:], axis=2) / (left[:, :, 0] + 1.0)
    right_part = jnp.sum(right[:, :, 1:] * right[:, :, 1:], axis=2) / (right[:, :, 0] + 1.0)
    total_part = jnp.sum(total[:, :, 1:] * total[:, :, 1:], axis=2) / (total[:, :, 0] + 1.0)
    gain = left_part + right_part - total_part
    best_gain = jnp.max(gain, axis=(1, 2))
    return histogram, best_gain
```

```python
import functools

import jax
import jax.numpy as jnp
from jax import lax
from jax.experimental import pallas as pl
from jax.experimental.pallas import tpu as pltpu
from jax.sharding import PartitionSpec as P

B = 256
HI = 4
LO = B // HI
LANES = 128
VMEM = 56 * 1024 * 1024
NT = (((1,), (1,)), ((), ()))


def triangle():
    row = lax.broadcasted_iota(jnp.int32, (B, B), 0)
    column = lax.broadcasted_iota(jnp.int32, (B, B), 1)
    return jnp.where(row <= column, 1.0, 0.0).astype(jnp.bfloat16)


def rank_kernel(honest_ref, destination_ref, slot_ref, target_ref, rank_ref, count_ref):
    nodes = slot_ref.shape[0]
    rows = honest_ref.shape[1]
    upper = triangle()
    index = lax.broadcasted_iota(jnp.int32, (nodes, B), 0)
    carry = jnp.zeros((nodes, 1), jnp.float32)
    for block in range(rows // B):
        span = pl.ds(block * B, B)
        named = destination_ref[:, span] == index
        target = jnp.sum(jnp.where(named, slot_ref[...], 0), axis=0, keepdims=True)
        active = honest_ref[:, span] == 0
        owned = jnp.where((target == index) & active, 1.0, 0.0)
        upto = jnp.dot(owned.astype(jnp.bfloat16), upper, preferred_element_type=jnp.float32) + carry
        rank = jnp.sum(owned * upto, axis=0, keepdims=True) - 1.0
        target_ref[:, span] = target.astype(jnp.float32)
        rank_ref[:, span] = rank
        carry = upto[:, B - 1 : B]
    count_ref[...] = jnp.broadcast_to(carry, count_ref.shape)


def ranks(honest, destination, node_slot):
    rows = honest.shape[0]
    nodes = node_slot.shape[0]
    return pl.pallas_call(
        rank_kernel,
        out_shape=(
            jax.ShapeDtypeStruct((1, rows), jnp.float32),
            jax.ShapeDtypeStruct((1, rows), jnp.float32),
            jax.ShapeDtypeStruct((nodes, LANES), jnp.float32),
        ),
        compiler_params=pltpu.CompilerParams(vmem_limit_bytes=VMEM),
    )(honest.reshape(1, rows), destination.reshape(1, rows), node_slot.reshape(nodes, 1))


def permute_kernel(capacity, local, parts, cov_ref, pseudo_ref, target_ref, rank_ref, *rest):
    outs, (payload, place) = rest[: parts + 1], rest[parts + 1 :]
    device = pl.program_id(0)
    features = cov_ref.shape[0]
    rows = cov_ref.shape[1]

    @pl.when(device == 0)
    def _():
        level = jnp.floor(cov_ref[...].astype(jnp.float32) * B) + 1.0
        payload[0:features, :] = level.astype(jnp.bfloat16)
        payload[features : features + 16, :] = pseudo_ref[...]

    step = 512
    for n in range(local):
        node = (device * local + n).astype(jnp.float32)
        for c in range(rows // step):
            span = pl.ds(c * step, step)
            key = jnp.where(target_ref[:, span] == node, rank_ref[:, span], -1.0)
            key = jnp.broadcast_to(key, (16, step)).astype(jnp.bfloat16)
            for j in range(capacity // 16):
                at = lax.broadcasted_iota(jnp.int32, (16, step), 0).astype(jnp.float32) + float(16 * j)
                hit = jnp.where(key == at.astype(jnp.bfloat16), jnp.bfloat16(1), jnp.bfloat16(0))
                place[n * capacity + 16 * j : n * capacity + 16 * j + 16, span] = hit
    moved = lax.dot_general(payload[...], place[...], NT, preferred_element_type=jnp.float32)
    moved = moved.astype(jnp.bfloat16)
    each = features // parts
    for k in range(parts):
        outs[k][0] = moved[k * each : (k + 1) * each]
    outs[parts][0] = moved[features:]


def permute(covariates, pseudo, target, rank, capacity, local, devices, parts):
    features, rows = covariates.shape
    width = local * capacity
    each = features // parts
    whole = lambda d: (0, 0)
    sizes = [each] * parts + [16]
    return pl.pallas_call(
        functools.partial(permute_kernel, capacity, local, parts),
        grid=(devices,),
        in_specs=[
            pl.BlockSpec((features, rows), whole),
            pl.BlockSpec((16, rows), whole),
            pl.BlockSpec((1, rows), whole),
            pl.BlockSpec((1, rows), whole),
        ],
        out_specs=[pl.BlockSpec((1, size, width), lambda d: (d, 0, 0)) for size in sizes],
        out_shape=[jax.ShapeDtypeStruct((devices, size, width), jnp.bfloat16) for size in sizes],
        scratch_shapes=[
            pltpu.VMEM((features + 16, rows), jnp.bfloat16),
            pltpu.VMEM((width, rows), jnp.bfloat16),
        ],
        compiler_params=pltpu.CompilerParams(vmem_limit_bytes=VMEM),
    )(covariates, pseudo, target, rank)


def gather_rows(arrived, node, capacity, store):
    devices = arrived.shape[0]
    head = capacity // LANES * LANES
    tail = capacity - head
    first = 0 if node == 0 else head + 2 * tail
    for s in range(devices):
        store(s * head, arrived[s, :, first : first + head].astype(jnp.float32))
    if tail:
        for i in range(devices // 2):
            one = arrived[2 * i, :, head : head + LANES].astype(jnp.float32)
            two = arrived[2 * i + 1, :, head : head + LANES].astype(jnp.float32)
            lane = lax.broadcasted_iota(jnp.int32, one.shape, 1)
            if node == 0:
                mixed = jnp.where(lane < tail, one, pltpu.roll(two, tail, 1))
            else:
                mixed = jnp.where(lane < tail, pltpu.roll(one, tail, 1), two)
            store(devices * head + i * LANES, mixed)


def histogram_kernel(capacity, local, chained, arrived, stats, *rest):
    if chained:
        rest = rest[1:]
    out_ref, best_ref, high, low, values, left_side, right_side = rest
    group = pl.program_id(0)
    rows = high.shape[2]

    @pl.when(group == 0)
    def _():
        best_ref[...] = jnp.full(best_ref.shape, -jnp.inf, jnp.float32)
        for n in range(local):

            def store(at, part):
                level = part - 1.0
                upper = jnp.floor(level * (1.0 / LO))
                span = slice(at, at + part.shape[1])
                high[n, :, span] = upper
                low[n, :, span] = level - upper * LO

            def store_values(at, part):
                values[n, :, at : at + part.shape[1]] = part.astype(jnp.bfloat16)

            gather_rows(arrived, n, capacity, store)
            gather_rows(stats, n, capacity, store_values)

    upper = triangle()
    step = 512
    sub = lax.broadcasted_iota(jnp.int32, (16, step), 0)
    subf = sub.astype(jnp.float32)
    zero, one = jnp.bfloat16(0), jnp.bfloat16(1)
    for n in range(local):
        for c in range(rows // step):
            span = pl.ds(c * step, step)
            stat = values[n, :, span]
            mixed = None
            for f in range(4):
                top = jnp.broadcast_to(high[n, pl.ds(group * 4 + f, 1), span], (16, step))
                bottom = jnp.broadcast_to(low[n, pl.ds(group * 4 + f, 1), span], (16, step)).astype(jnp.bfloat16)
                mixed = top if f == 0 else jnp.where(sub >= 4 * f, top, mixed)
                top = top.astype(jnp.bfloat16)
                for h in range(HI):
                    left_side[(f * HI + h) * 16 : (f * HI + h + 1) * 16, span] = jnp.where(top == jnp.bfloat16(h), stat, zero)
                for j in range(LO // 16):
                    at = (subf + float(16 * j)).astype(jnp.bfloat16)
                    right_side[f * LO + 16 * j : f * LO + 16 * j + 16, span] = jnp.where(bottom == at, one, zero)
            wanted = (sub % 4).astype(jnp.float32)
            left_side[256:272, span] = jnp.where(mixed == wanted, 1.0, 0.0).astype(jnp.bfloat16)
        sums = lax.dot_general(left_side[...], right_side[...], NT, preferred_element_type=jnp.float32)
        pieces = []
        weights = []
        for f in range(4):
            lanes = slice(f * LO, (f + 1) * LO)
            piece = jnp.concatenate([sums[(f * HI + h) * 16 : (f * HI + h + 1) * 16, lanes] for h in range(HI)], axis=1)
            weight = jnp.concatenate([sums[256 + f * HI + h : 257 + f * HI + h, lanes] for h in range(HI)], axis=1)
            out_ref[n, f, 0:1] = weight
            out_ref[n, f, 1:17] = piece
            pieces.append(piece)
            weights.append(weight)
        table = jnp.concatenate(pieces + weights + [jnp.zeros((4, B), jnp.float32)], axis=0)
        first = table.astype(jnp.bfloat16)
        table = table - first.astype(jnp.float32)
        second = table.astype(jnp.bfloat16)
        third = (table - second.astype(jnp.float32)).astype(jnp.bfloat16)
        left = (
            jnp.dot(third, upper, preferred_element_type=jnp.float32)
            + jnp.dot(second, upper, preferred_element_type=jnp.float32)
            + jnp.dot(first, upper, preferred_element_type=jnp.float32)
        )
        total = left[:, B - 1 : B]
        right = total - left
        for f in range(4):
            span = slice(16 * f, 16 * f + 16)
            count = slice(64 + f, 65 + f)
            squared = lambda side: jnp.sum(side[span] * side[span], axis=0, keepdims=True) / (side[count] + 1.0)
            gain = squared(left) + squared(right) - squared(total)
            best_ref[n : n + 1, :] = jnp.maximum(best_ref[n : n + 1, :], gain)


def histogram_part(arrived, stats, previous, part, features, capacity, local):
    devices, each, width = arrived.shape
    rows = devices * capacity
    groups = each // 4
    whole = lambda g: (0, 0, 0)
    in_specs = [pl.BlockSpec((devices, each, width), whole), pl.BlockSpec((devices, 16, width), whole)]
    operands = [arrived, stats]
    chained = previous is not None
    if chained:
        in_specs.append(pl.BlockSpec(memory_space=pl.ANY))
        operands.append(previous)
    return pl.pallas_call(
        functools.partial(histogram_kernel, capacity, local, chained),
        grid=(groups,),
        in_specs=in_specs,
        out_specs=[
            pl.BlockSpec((local, 4, 17, B), lambda g: (0, part * groups + g, 0, 0)),
            pl.BlockSpec((local, B), lambda g: (0, 0)),
        ],
        out_shape=[
            jax.ShapeDtypeStruct((local, features, 17, B), jnp.float32),
            jax.ShapeDtypeStruct((local, B), jnp.float32),
        ],
        scratch_shapes=[
            pltpu.VMEM((local, each, rows), jnp.float32),
            pltpu.VMEM((local, each, rows), jnp.float32),
            pltpu.VMEM((local, 16, rows), jnp.bfloat16),
            pltpu.VMEM((272, rows), jnp.bfloat16),
            pltpu.VMEM((256, rows), jnp.bfloat16),
        ],
        input_output_aliases={2: 0} if chained else {},
        compiler_params=pltpu.CompilerParams(vmem_limit_bytes=VMEM),
        cost_estimate=pl.CostEstimate(
            flops=2 * local * groups * 272 * 256 * rows, bytes_accessed=arrived.size * 2, transcendentals=0
        ),
    )(*operands)


def finish(sent, features, capacity, local):
    parts = len(sent) - 1
    swap = lambda block: lax.all_to_all(block, "node", split_axis=0, concat_axis=0, tiled=True)
    stats = swap(sent[parts])
    arrived = [swap(block) for block in sent[:parts]]
    histogram, best = None, None
    for k in range(parts):
        histogram, part_best = histogram_part(arrived[k], stats, histogram, k, features, capacity, local)
        best = part_best if best is None else jnp.maximum(best, part_best)
    return histogram, best


def on_device(covariates, pseudo, honest, destination, node_slot):
    features, rows = covariates.shape
    devices = lax.axis_size("node")
    nodes = node_slot.shape[0]
    local = nodes // devices
    most = 2 * rows // nodes
    parts = max(1, min(4, features // 16))
    small = most - 64 if most % LANES == 0 and most > LANES else most
    target, rank, count = ranks(honest, destination, node_slot)

    def route(capacity):
        return permute(covariates, pseudo, target, rank, capacity, local, devices, parts)

    if small < most:
        over = lax.pmax(jnp.max(count), "node") > small
        quick = route(small)
        histogram, best = lax.cond(
            over,
            lambda: tuple(finish(route(most), features, most, local)),
            lambda: tuple(finish(quick, features, small, local)),
        )
    else:
        histogram, best = finish(route(most), features, most, local)
    best_gain = lax.pmax(jnp.max(best, axis=1), "feat")
    return (histogram, best_gain)


def solution(mesh):
    placed = (P("feat", "node"), P(None, "node"), P("node"), P("node", None), P())
    return jax.shard_map(
        on_device,
        mesh=mesh,
        in_specs=placed,
        out_specs=(P("node", "feat", None, None), P("node")),
        check_vma=False,
    )
```

```python
import functools
import math

import jax
import jax.numpy as jnp
from jax import lax
from jax.experimental import pallas as pl
from jax.experimental.pallas import tpu as pltpu
from jax.sharding import PartitionSpec as P

B = 256
HI = 4
LO = B // HI
LANES = 128
POISON = 512.0
VMEM = 48 * 1024 * 1024
NT = (((1,), (1,)), ((), ()))


def triangle():
    row = lax.broadcasted_iota(jnp.int32, (B, B), 0)
    column = lax.broadcasted_iota(jnp.int32, (B, B), 1)
    return jnp.where(row <= column, 1.0, 0.0).astype(jnp.bfloat16)


def rank_kernel(honest_ref, destination_ref, slot_ref, target_ref, rank_ref, count_ref):
    nodes = slot_ref.shape[0]
    rows = honest_ref.shape[1]
    upper = triangle()
    index = lax.broadcasted_iota(jnp.int32, (nodes, B), 0)
    carry = jnp.zeros((nodes, 1), jnp.float32)
    for block in range(rows // B):
        span = pl.ds(block * B, B)
        named = destination_ref[:, span] == index
        target = jnp.sum(jnp.where(named, slot_ref[...], 0), axis=0, keepdims=True)
        active = honest_ref[:, span] == 0
        owned = jnp.where((target == index) & active, 1.0, 0.0)
        upto = jnp.dot(owned.astype(jnp.bfloat16), upper, preferred_element_type=jnp.float32) + carry
        rank = jnp.sum(owned * upto, axis=0, keepdims=True) - 1.0
        target_ref[:, span] = target.astype(jnp.float32)
        rank_ref[:, span] = rank
        carry = upto[:, B - 1 : B]
    count_ref[...] = jnp.broadcast_to(carry, count_ref.shape)


def ranks(honest, destination, node_slot):
    rows = honest.shape[0]
    nodes = node_slot.shape[0]
    return pl.pallas_call(
        rank_kernel,
        out_shape=(
            jax.ShapeDtypeStruct((1, rows), jnp.float32),
            jax.ShapeDtypeStruct((1, rows), jnp.float32),
            jax.ShapeDtypeStruct((nodes, LANES), jnp.float32),
        ),
        compiler_params=pltpu.CompilerParams(vmem_limit_bytes=VMEM),
    )(honest.reshape(1, rows), destination.reshape(1, rows), node_slot.reshape(nodes, 1))


def permute_kernel(capacity, local, pair, cov_ref, pseudo_ref, target_ref, rank_ref, count_ref, *rest):
    outs, payload, places = rest[: -1 - pair * local], rest[-1 - pair * local], rest[-pair * local :]
    group = pl.program_id(0)
    rows = cov_ref.shape[1]
    head = capacity // LANES * LANES
    tail = capacity - head

    @pl.when(group == 0)
    def _():
        payload[0:16, :] = pseudo_ref[...]
        level = jnp.floor(cov_ref[...].astype(jnp.float32) * B) + 1.0
        payload[16:, :] = level.astype(jnp.bfloat16)

    over = jnp.max(count_ref[...], axis=0, keepdims=True)[:, 0:1] > float(capacity)
    step = math.gcd(rows, 512)
    for d in range(pair):
        for n in range(local):
            place = places[d * local + n]
            node = ((group * pair + d) * local + n).astype(jnp.float32)
            for c in range(rows // step):
                span = pl.ds(c * step, step)
                key = jnp.where(target_ref[:, span] == node, rank_ref[:, span], -1.0)
                key = jnp.broadcast_to(key, (16, step)).astype(jnp.bfloat16)
                for j in range(capacity // 16):
                    at = lax.broadcasted_iota(jnp.int32, (16, step), 0).astype(jnp.float32) + float(16 * j)
                    hit = jnp.where(key == at.astype(jnp.bfloat16), jnp.bfloat16(1), jnp.bfloat16(0))
                    place[16 * j : 16 * j + 16, span] = hit
            moved = lax.dot_general(payload[...], place[...], NT, preferred_element_type=jnp.float32)
            first = 0
            for out in outs:
                size = out.shape[1]
                part = moved[first : first + size]
                if first == 0:
                    part = jnp.where(over, POISON, part)
                part = part.astype(jnp.bfloat16)
                out[d, :, n * head : (n + 1) * head] = part[:, :head]
                if tail:
                    at = local * head + n * tail
                    out[d, :, at : at + tail] = part[:, head:]
                first += size


def permute(covariates, pseudo, target, rank, count, capacity, local, devices, sizes):
    features, rows = covariates.shape
    width = local * capacity
    pair = 2 if devices % 2 == 0 else 1
    whole = lambda d: (0, 0)
    return pl.pallas_call(
        functools.partial(permute_kernel, capacity, local, pair),
        grid=(devices // pair,),
        in_specs=[
            pl.BlockSpec((features, rows), whole),
            pl.BlockSpec((16, rows), whole),
            pl.BlockSpec((1, rows), whole),
            pl.BlockSpec((1, rows), whole),
            pl.BlockSpec(count.shape, whole),
        ],
        out_specs=[pl.BlockSpec((pair, size, width), lambda d: (d, 0, 0)) for size in sizes],
        out_shape=[jax.ShapeDtypeStruct((devices, size, width), jnp.bfloat16) for size in sizes],
        scratch_shapes=[pltpu.VMEM((features + 16, rows), jnp.bfloat16)]
        + [pltpu.VMEM((capacity, rows), jnp.bfloat16)] * (pair * local),
        compiler_params=pltpu.CompilerParams(vmem_limit_bytes=VMEM),
    )(covariates, pseudo, target, rank, count)


def gather_rows(arrived, first, size, node, capacity, local, store):
    devices = arrived.shape[0]
    head = capacity // LANES * LANES
    tail = capacity - head
    span = slice(first, first + size)
    for s in range(devices):
        store(s * head, arrived[s, span, node * head : (node + 1) * head].astype(jnp.float32))
    if tail:
        each = LANES // tail
        lane = lax.broadcasted_iota(jnp.int32, (size, local * tail), 1)
        for i in range(devices // each):
            columns = []
            for j in range(each):
                block = arrived[each * i + j, span, local * head : local * capacity].astype(jnp.float32)
                columns.append(block[:, node * tail : (node + 1) * tail])
            store(devices * head + i * LANES, jnp.concatenate(columns, axis=1))


def histogram_kernel(capacity, local, first, size, chained, *refs):
    if chained:
        arrived, stats, _, before_ref, out_ref, best_ref, high, low, values = refs[:9]
        sides = refs[9:]
    else:
        arrived, out_ref, best_ref, high, low, values = refs[:6]
        stats = arrived
        sides = refs[6:]
    group = pl.program_id(0)
    rows = high.shape[2]

    @pl.when(group == 0)
    def _():
        if chained:
            best_ref[...] = before_ref[...]
        else:
            best_ref[...] = jnp.full(best_ref.shape, -jnp.inf, jnp.float32)
        for n in range(local):

            def store(at, part):
                level = part - 1.0
                upper = jnp.floor(level * (1.0 / LO))
                span = slice(at, at + part.shape[1])
                high[n, :, span] = upper
                low[n, :, span] = level - upper * LO

            def store_values(at, part):
                values[n, :, at : at + part.shape[1]] = part.astype(jnp.bfloat16)

            gather_rows(arrived, first, size, n, capacity, local, store)
            gather_rows(stats, 0, 16, n, capacity, local, store_values)

    upper = triangle()
    step = math.gcd(rows, 512)
    sub = lax.broadcasted_iota(jnp.int32, (16, step), 0)
    subf = sub.astype(jnp.float32)
    wanted = (sub % 4).astype(jnp.float32)
    zero, one = jnp.bfloat16(0), jnp.bfloat16(1)
    for turn in range(2 * local):
        q, n = turn // local, turn % local
        left_side, right_side = sides[2 * turn], sides[2 * turn + 1]
        for c in range(rows // step):
            span = pl.ds(c * step, step)
            stat = values[n, :, span]
            mixed = None
            for f in range(4):
                row = pl.ds(group * 8 + q * 4 + f, 1)
                top = jnp.broadcast_to(high[n, row, span], (16, step))
                bottom = jnp.broadcast_to(low[n, row, span], (16, step)).astype(jnp.bfloat16)
                mixed = top if f == 0 else jnp.where(sub >= 4 * f, top, mixed)
                top = top.astype(jnp.bfloat16)
                for h in range(HI):
                    at = (f * HI + h) * 16
                    left_side[at : at + 16, span] = jnp.where(top == jnp.bfloat16(h), stat, zero)
                for j in range(LO // 16):
                    at = (subf + float(16 * j)).astype(jnp.bfloat16)
                    right_side[f * LO + 16 * j : f * LO + 16 * j + 16, span] = jnp.where(bottom == at, one, zero)
            left_side[256:272, span] = jnp.where(mixed == wanted, 1.0, 0.0).astype(jnp.bfloat16)
        sums = lax.dot_general(left_side[...], right_side[...], NT, preferred_element_type=jnp.float32)
        pieces = []
        weights = []
        for f in range(4):
            lanes = slice(f * LO, (f + 1) * LO)
            piece = jnp.concatenate([sums[(f * HI + h) * 16 : (f * HI + h + 1) * 16, lanes] for h in range(HI)], axis=1)
            weight = jnp.concatenate([sums[256 + f * HI + h : 257 + f * HI + h, lanes] for h in range(HI)], axis=1)
            out_ref[n, 0, q * 4 + f : q * 4 + f + 1, :] = weight
            out_ref[n, 1:17, q * 4 + f, :] = piece
            pieces.append(piece)
            weights.append(weight)
        table = jnp.concatenate(pieces + weights + [jnp.zeros((4, B), jnp.float32)], axis=0)
        one_part = table.astype(jnp.bfloat16)
        table = table - one_part.astype(jnp.float32)
        two_part = table.astype(jnp.bfloat16)
        three_part = (table - two_part.astype(jnp.float32)).astype(jnp.bfloat16)
        left = (
            jnp.dot(three_part, upper, preferred_element_type=jnp.float32)
            + jnp.dot(two_part, upper, preferred_element_type=jnp.float32)
            + jnp.dot(one_part, upper, preferred_element_type=jnp.float32)
        )
        total = left[:, B - 1 : B]
        right = total - left
        for f in range(4):
            span = slice(16 * f, 16 * f + 16)
            count = slice(64 + f, 65 + f)
            squared = lambda side: jnp.sum(side[span] * side[span], axis=0, keepdims=True) / (side[count] + 1.0)
            gain = squared(left) + squared(right) - squared(total)
            best_ref[n : n + 1, :] = jnp.maximum(best_ref[n : n + 1, :], gain)


def histogram_part(arrived, stats, previous, first, size, offset, features, capacity, local):
    devices, height, width = arrived.shape
    rows = devices * capacity
    groups = size // 8
    whole = lambda g: (0, 0, 0)
    chained = previous is not None
    in_specs = [pl.BlockSpec((devices, height, width), whole)]
    operands = [arrived]
    if chained:
        in_specs += [
            pl.BlockSpec((devices, 16, width), whole),
            pl.BlockSpec(memory_space=pl.ANY),
            pl.BlockSpec((local, B), lambda g: (0, 0)),
        ]
        operands += [stats, previous[0], previous[1]]
    return pl.pallas_call(
        functools.partial(histogram_kernel, capacity, local, first, size, chained),
        grid=(groups,),
        in_specs=in_specs,
        out_specs=[
            pl.BlockSpec((local, 17, 8, B), lambda g: (0, 0, offset // 8 + g, 0)),
            pl.BlockSpec((local, B), lambda g: (0, 0)),
        ],
        out_shape=[
            jax.ShapeDtypeStruct((local, 17, features, B), jnp.float32),
            jax.ShapeDtypeStruct((local, B), jnp.float32),
        ],
        scratch_shapes=[
            pltpu.VMEM((local, size, rows), jnp.float32),
            pltpu.VMEM((local, size, rows), jnp.float32),
            pltpu.VMEM((local, 16, rows), jnp.bfloat16),
        ]
        + [pltpu.VMEM((272, rows), jnp.bfloat16), pltpu.VMEM((256, rows), jnp.bfloat16)] * (2 * local),
        input_output_aliases={2: 0} if chained else {},
        compiler_params=pltpu.CompilerParams(vmem_limit_bytes=VMEM),
        cost_estimate=pl.CostEstimate(
            flops=4 * local * groups * 272 * 256 * rows, bytes_accessed=arrived.size * 2, transcendentals=0
        ),
    )(*operands)


def swap(block):
    return lax.all_to_all(block, "node", split_axis=0, concat_axis=0, tiled=True)


def finish(first_arrived, sent, features, capacity, local):
    size = first_arrived.shape[1] - 16
    result = histogram_part(first_arrived, None, None, 16, size, 0, features, capacity, local)
    for block in sent:
        arrived = swap(block)
        result = histogram_part(
            arrived, first_arrived, result, 0, block.shape[1], size, features, capacity, local
        )
        size += block.shape[1]
    return tuple(result)


def on_device(covariates, pseudo, honest, destination, node_slot):
    features, rows = covariates.shape
    devices = lax.axis_size("node")
    nodes = node_slot.shape[0]
    local = nodes // devices
    most = 2 * rows // nodes
    early = features // 8 * 3
    early = early if early % 16 == 0 else features
    sizes = [16 + early] + ([features - early] if early < features else [])
    small = most - 96 if most % LANES == 0 and most > LANES else most
    target, rank, count = ranks(honest, destination, node_slot)

    def route(capacity):
        return permute(covariates, pseudo, target, rank, count, capacity, local, devices, sizes)

    def full():
        sent = route(most)
        return finish(swap(sent[0]), sent[1:], features, most, local)

    if small < most:
        sent = route(small)
        arrived = swap(sent[0])
        over = jnp.max(arrived[:, 0, 0]) > POISON / 2
        histogram, best = lax.cond(over, full, lambda: finish(arrived, sent[1:], features, small, local))
    else:
        histogram, best = full()
    best_gain = lax.pmax(jnp.max(best, axis=1), "feat")
    return (jnp.transpose(histogram, (0, 2, 1, 3)), best_gain)


def solution(mesh):
    placed = (P("feat", "node"), P(None, "node"), P("node"), P("node", None), P())
    return jax.shard_map(
        on_device,
        mesh=mesh,
        in_specs=placed,
        out_specs=(P("node", "feat", None, None), P("node")),
        check_vma=False,
    )
```

```python
import functools
import math

import jax
import jax.numpy as jnp
from jax import lax
from jax.experimental import pallas as pl
from jax.experimental.pallas import tpu as pltpu
from jax.sharding import PartitionSpec as P

B = 256
HI = 4
LO = B // HI
LANES = 128
POISON = 512.0
VMEM = 48 * 1024 * 1024
NT = (((1,), (1,)), ((), ()))


def triangle():
    row = lax.broadcasted_iota(jnp.int32, (B, B), 0)
    column = lax.broadcasted_iota(jnp.int32, (B, B), 1)
    return jnp.where(row <= column, 1.0, 0.0).astype(jnp.bfloat16)


def rank_kernel(honest_ref, destination_ref, slot_ref, target_ref, rank_ref, count_ref):
    nodes = slot_ref.shape[0]
    rows = honest_ref.shape[1]
    upper = triangle()
    index = lax.broadcasted_iota(jnp.int32, (nodes, B), 0)
    carry = jnp.zeros((nodes, 1), jnp.float32)
    for block in range(rows // B):
        span = pl.ds(block * B, B)
        named = destination_ref[:, span] == index
        target = jnp.sum(jnp.where(named, slot_ref[...], 0), axis=0, keepdims=True)
        active = honest_ref[:, span] == 0
        owned = jnp.where((target == index) & active, 1.0, 0.0)
        upto = jnp.dot(owned.astype(jnp.bfloat16), upper, preferred_element_type=jnp.float32) + carry
        rank = jnp.sum(owned * upto, axis=0, keepdims=True) - 1.0
        target_ref[:, span] = target.astype(jnp.float32)
        rank_ref[:, span] = rank
        carry = upto[:, B - 1 : B]
    count_ref[...] = jnp.broadcast_to(carry, count_ref.shape)


def ranks(honest, destination, node_slot):
    rows = honest.shape[0]
    nodes = node_slot.shape[0]
    return pl.pallas_call(
        rank_kernel,
        out_shape=(
            jax.ShapeDtypeStruct((1, rows), jnp.float32),
            jax.ShapeDtypeStruct((1, rows), jnp.float32),
            jax.ShapeDtypeStruct((nodes, LANES), jnp.float32),
        ),
        compiler_params=pltpu.CompilerParams(vmem_limit_bytes=VMEM),
    )(honest.reshape(1, rows), destination.reshape(1, rows), node_slot.reshape(nodes, 1))


def permute_kernel(capacity, local, pair, cov_ref, pseudo_ref, target_ref, rank_ref, count_ref, *rest):
    outs, payload, places = rest[: -1 - pair * local], rest[-1 - pair * local], rest[-pair * local :]
    group = pl.program_id(0)
    rows = cov_ref.shape[1]
    head = capacity // LANES * LANES
    tail = capacity - head

    @pl.when(group == 0)
    def _():
        payload[0:16, :] = pseudo_ref[...]
        level = jnp.floor(cov_ref[...].astype(jnp.float32) * B) + 1.0
        payload[16:, :] = level.astype(jnp.bfloat16)

    over = jnp.max(count_ref[...], axis=0, keepdims=True)[:, 0:1] > float(capacity)
    step = math.gcd(rows, 512)
    for d in range(pair):
        for n in range(local):
            place = places[d * local + n]
            node = ((group * pair + d) * local + n).astype(jnp.float32)
            for c in range(rows // step):
                span = pl.ds(c * step, step)
                key = jnp.where(target_ref[:, span] == node, rank_ref[:, span], -1.0)
                key = jnp.broadcast_to(key, (16, step)).astype(jnp.bfloat16)
                for j in range(capacity // 16):
                    at = lax.broadcasted_iota(jnp.int32, (16, step), 0).astype(jnp.float32) + float(16 * j)
                    hit = jnp.where(key == at.astype(jnp.bfloat16), jnp.bfloat16(1), jnp.bfloat16(0))
                    place[16 * j : 16 * j + 16, span] = hit
            moved = lax.dot_general(payload[...], place[...], NT, preferred_element_type=jnp.float32)
            first = 0
            for out in outs:
                size = out.shape[1]
                part = moved[first : first + size]
                if first == 0:
                    part = jnp.where(over, POISON, part)
                part = part.astype(jnp.bfloat16)
                out[d, :, n * head : (n + 1) * head] = part[:, :head]
                if tail:
                    at = local * head + n * tail
                    out[d, :, at : at + tail] = part[:, head:]
                first += size


def permute(covariates, pseudo, target, rank, count, capacity, local, devices, sizes):
    features, rows = covariates.shape
    width = local * capacity
    pair = 2 if devices % 2 == 0 else 1
    whole = lambda d: (0, 0)
    return pl.pallas_call(
        functools.partial(permute_kernel, capacity, local, pair),
        grid=(devices // pair,),
        in_specs=[
            pl.BlockSpec((features, rows), whole),
            pl.BlockSpec((16, rows), whole),
            pl.BlockSpec((1, rows), whole),
            pl.BlockSpec((1, rows), whole),
            pl.BlockSpec(count.shape, whole),
        ],
        out_specs=[pl.BlockSpec((pair, size, width), lambda d: (d, 0, 0)) for size in sizes],
        out_shape=[jax.ShapeDtypeStruct((devices, size, width), jnp.bfloat16) for size in sizes],
        scratch_shapes=[pltpu.VMEM((features + 16, rows), jnp.bfloat16)]
        + [pltpu.VMEM((capacity, rows), jnp.bfloat16)] * (pair * local),
        compiler_params=pltpu.CompilerParams(vmem_limit_bytes=VMEM),
    )(covariates, pseudo, target, rank, count)


def gather_rows(arrived, first, size, node, capacity, local, store):
    devices = arrived.shape[0]
    head = capacity // LANES * LANES
    tail = capacity - head
    span = slice(first, first + size)
    for s in range(devices):
        store(s * head, arrived[s, span, node * head : (node + 1) * head].astype(jnp.float32))
    if tail:
        each = LANES // tail
        lane = lax.broadcasted_iota(jnp.int32, (size, local * tail), 1)
        for i in range(devices // each):
            columns = []
            for j in range(each):
                block = arrived[each * i + j, span, local * head : local * capacity].astype(jnp.float32)
                columns.append(block[:, node * tail : (node + 1) * tail])
            store(devices * head + i * LANES, jnp.concatenate(columns, axis=1))


def histogram_kernel(capacity, local, first, size, chained, *refs):
    if chained:
        arrived, stats, _, before_ref, out_ref, best_ref, high, low, values = refs
    else:
        arrived, out_ref, best_ref, high, low, values = refs
        stats = arrived
    group = pl.program_id(0)
    rows = high.shape[2]

    @pl.when(group == 0)
    def _():
        if chained:
            best_ref[...] = before_ref[...]
        else:
            best_ref[...] = jnp.full(best_ref.shape, -jnp.inf, jnp.float32)
        for n in range(local):

            def store(at, part):
                level = part - 1.0
                upper = jnp.floor(level * (1.0 / LO))
                span = slice(at, at + part.shape[1])
                high[n, :, span] = upper
                low[n, :, span] = level - upper * LO

            def store_values(at, part):
                values[n, :, at : at + part.shape[1]] = part.astype(jnp.bfloat16)

            gather_rows(arrived, first, size, n, capacity, local, store)
            gather_rows(stats, 0, 16, n, capacity, local, store_values)

    upper = triangle()
    step = math.gcd(rows, 512)
    sub = lax.broadcasted_iota(jnp.int32, (16, step), 0)
    subf = sub.astype(jnp.float32)
    wanted = (sub % 4).astype(jnp.float32)
    zero, one = jnp.bfloat16(0), jnp.bfloat16(1)
    tables = []
    for turn in range(2 * local):
        q, n = turn // local, turn % local
        sums = None
        for c in range(rows // step):
            span = pl.ds(c * step, step)
            stat = values[n, :, span]
            mixed = None
            left_side, right_side = [], []
            for f in range(4):
                row = pl.ds(group * 8 + q * 4 + f, 1)
                top = jnp.broadcast_to(high[n, row, span], (16, step))
                bottom = jnp.broadcast_to(low[n, row, span], (16, step)).astype(jnp.bfloat16)
                mixed = top if f == 0 else jnp.where(sub >= 4 * f, top, mixed)
                top = top.astype(jnp.bfloat16)
                for h in range(HI):
                    left_side.append(jnp.where(top == jnp.bfloat16(h), stat, zero))
                for j in range(LO // 16):
                    at = (subf + float(16 * j)).astype(jnp.bfloat16)
                    right_side.append(jnp.where(bottom == at, one, zero))
            left_side.append(jnp.where(mixed == wanted, 1.0, 0.0).astype(jnp.bfloat16))
            product = lax.dot_general(
                jnp.concatenate(left_side, axis=0),
                jnp.concatenate(right_side, axis=0),
                NT,
                preferred_element_type=jnp.float32,
            )
            sums = product if sums is None else sums + product
        weights = []
        for f in range(4):
            lanes = slice(f * LO, (f + 1) * LO)
            piece = jnp.concatenate([sums[(f * HI + h) * 16 : (f * HI + h + 1) * 16, lanes] for h in range(HI)], axis=1)
            weight = jnp.concatenate([sums[256 + f * HI + h : 257 + f * HI + h, lanes] for h in range(HI)], axis=1)
            out_ref[n, 0, q * 4 + f : q * 4 + f + 1, :] = weight
            out_ref[n, 1:17, q * 4 + f, :] = piece
            tables.append(piece)
            weights.append(weight)
        tables.append(jnp.concatenate(weights + [jnp.zeros((4, B), jnp.float32)], axis=0))
    table = jnp.concatenate(tables, axis=0)
    one_part = table.astype(jnp.bfloat16)
    table = table - one_part.astype(jnp.float32)
    two_part = table.astype(jnp.bfloat16)
    three_part = (table - two_part.astype(jnp.float32)).astype(jnp.bfloat16)
    left = (
        jnp.dot(three_part, upper, preferred_element_type=jnp.float32)
        + jnp.dot(two_part, upper, preferred_element_type=jnp.float32)
        + jnp.dot(one_part, upper, preferred_element_type=jnp.float32)
    )
    total = left[:, B - 1 : B]
    right = total - left
    for turn in range(2 * local):
        n = turn % local
        for f in range(4):
            span = slice(72 * turn + 16 * f, 72 * turn + 16 * f + 16)
            count = slice(72 * turn + 64 + f, 72 * turn + 65 + f)
            squared = lambda side: jnp.sum(side[span] * side[span], axis=0, keepdims=True) / (side[count] + 1.0)
            gain = squared(left) + squared(right) - squared(total)
            best_ref[n : n + 1, :] = jnp.maximum(best_ref[n : n + 1, :], gain)


def histogram_part(arrived, stats, previous, first, size, offset, features, capacity, local):
    devices, height, width = arrived.shape
    rows = devices * capacity
    groups = size // 8
    whole = lambda g: (0, 0, 0)
    chained = previous is not None
    in_specs = [pl.BlockSpec((devices, height, width), whole)]
    operands = [arrived]
    if chained:
        in_specs += [
            pl.BlockSpec((devices, 16, width), whole),
            pl.BlockSpec(memory_space=pl.ANY),
            pl.BlockSpec((local, B), lambda g: (0, 0)),
        ]
        operands += [stats, previous[0], previous[1]]
    return pl.pallas_call(
        functools.partial(histogram_kernel, capacity, local, first, size, chained),
        grid=(groups,),
        in_specs=in_specs,
        out_specs=[
            pl.BlockSpec((local, 17, 8, B), lambda g: (0, 0, offset // 8 + g, 0)),
            pl.BlockSpec((local, B), lambda g: (0, 0)),
        ],
        out_shape=[
            jax.ShapeDtypeStruct((local, 17, features, B), jnp.float32),
            jax.ShapeDtypeStruct((local, B), jnp.float32),
        ],
        scratch_shapes=[
            pltpu.VMEM((local, size, rows), jnp.float32),
            pltpu.VMEM((local, size, rows), jnp.float32),
            pltpu.VMEM((local, 16, rows), jnp.bfloat16),
        ],
        input_output_aliases={2: 0} if chained else {},
        compiler_params=pltpu.CompilerParams(vmem_limit_bytes=VMEM),
        cost_estimate=pl.CostEstimate(
            flops=4 * local * groups * 272 * 256 * rows, bytes_accessed=arrived.size * 2, transcendentals=0
        ),
    )(*operands)


def swap(block):
    return lax.all_to_all(block, "node", split_axis=0, concat_axis=0, tiled=True)


def finish(first_arrived, sent, features, capacity, local):
    size = first_arrived.shape[1] - 16
    result = histogram_part(first_arrived, None, None, 16, size, 0, features, capacity, local)
    for block in sent:
        arrived = swap(block)
        result = histogram_part(
            arrived, first_arrived, result, 0, block.shape[1], size, features, capacity, local
        )
        size += block.shape[1]
    return tuple(result)


def on_device(covariates, pseudo, honest, destination, node_slot):
    features, rows = covariates.shape
    devices = lax.axis_size("node")
    nodes = node_slot.shape[0]
    local = nodes // devices
    most = 2 * rows // nodes
    early = features // 2
    early = early if early % 16 == 0 else features
    sizes = [16 + early] + ([features - early] if early < features else [])
    small = most - 96 if most % LANES == 0 and most > LANES else most
    target, rank, count = ranks(honest, destination, node_slot)

    def route(capacity):
        return permute(covariates, pseudo, target, rank, count, capacity, local, devices, sizes)

    def full():
        sent = route(most)
        return finish(swap(sent[0]), sent[1:], features, most, local)

    if small < most:
        sent = route(small)
        arrived = swap(sent[0])
        over = jnp.max(arrived[:, 0, 0]) > POISON / 2
        histogram, best = lax.cond(over, full, lambda: finish(arrived, sent[1:], features, small, local))
    else:
        histogram, best = full()
    best_gain = lax.pmax(jnp.max(best, axis=1), "feat")
    return (jnp.transpose(histogram, (0, 2, 1, 3)), best_gain)


def solution(mesh):
    placed = (P("feat", "node"), P(None, "node"), P("node"), P("node", None), P())
    return jax.shard_map(
        on_device,
        mesh=mesh,
        in_specs=placed,
        out_specs=(P("node", "feat", None, None), P("node")),
        check_vma=False,
    )
```

```python
import functools
import math

import jax
import jax.numpy as jnp
from jax import lax
from jax.experimental import pallas as pl
from jax.experimental.pallas import tpu as pltpu
from jax.sharding import PartitionSpec as P

B = 256
HI = 4
LO = B // HI
LANES = 128
POISON = 512.0
VMEM = 48 * 1024 * 1024
NT = (((1,), (1,)), ((), ()))


def triangle():
    row = lax.broadcasted_iota(jnp.int32, (B, B), 0)
    column = lax.broadcasted_iota(jnp.int32, (B, B), 1)
    return jnp.where(row <= column, 1.0, 0.0).astype(jnp.bfloat16)


def rank_rows(honest_ref, destination_ref, slot_ref, target_ref, rank_ref, count_ref):
    nodes = slot_ref.shape[1]
    rows = honest_ref.shape[1]
    upper = triangle()
    across = lax.broadcasted_iota(jnp.int32, (nodes, nodes), 0) == lax.broadcasted_iota(jnp.int32, (nodes, nodes), 1)
    slots = jnp.sum(jnp.where(across, slot_ref[...].astype(jnp.float32), 0.0), axis=1, keepdims=True)
    index = lax.broadcasted_iota(jnp.int32, (nodes, B), 0)
    carry = jnp.zeros((nodes, 1), jnp.float32)
    for block in range(rows // B):
        span = pl.ds(block * B, B)
        named = destination_ref[:, span] == index
        target = jnp.sum(jnp.where(named, slots, 0.0), axis=0, keepdims=True)
        active = honest_ref[:, span] == 0
        owned = jnp.where((target == index.astype(jnp.float32)) & active, 1.0, 0.0)
        upto = jnp.dot(owned.astype(jnp.bfloat16), upper, preferred_element_type=jnp.float32) + carry
        target_ref[:, span] = target
        rank_ref[:, span] = jnp.sum(owned * upto, axis=0, keepdims=True) - 1.0
        carry = upto[:, B - 1 : B]
    count_ref[...] = jnp.broadcast_to(carry, count_ref.shape)


def permute_kernel(capacity, local, pair, cov_ref, pseudo_ref, honest_ref, destination_ref, slot_ref, *rest):
    outs, (payload, target_ref, rank_ref, count_ref) = rest[:-4], rest[-4:]
    group = pl.program_id(0)
    rows = cov_ref.shape[1]
    head = capacity // LANES * LANES
    tail = capacity - head

    @pl.when(group == 0)
    def _():
        payload[0:16, :] = pseudo_ref[...]
        level = jnp.floor(cov_ref[...].astype(jnp.float32) * B) + 1.0
        payload[16:, :] = level.astype(jnp.bfloat16)
        rank_rows(honest_ref, destination_ref, slot_ref, target_ref, rank_ref, count_ref)

    over = jnp.max(count_ref[...], axis=0, keepdims=True)[:, 0:1] > float(capacity)
    step = math.gcd(rows, 512)
    sub = lax.broadcasted_iota(jnp.int32, (16, step), 0).astype(jnp.float32)
    moved = None
    for c in range(rows // step):
        span = pl.ds(c * step, step)
        target, rank = target_ref[:, span], rank_ref[:, span]
        heads, tails = [], []
        for i in range(pair * local):
            node = (group * pair * local + i).astype(jnp.float32)
            key = jnp.where(target == node, rank, -1.0)
            key = jnp.broadcast_to(key, (16, step)).astype(jnp.bfloat16)
            for j in range(capacity // 16):
                at = (sub + float(16 * j)).astype(jnp.bfloat16)
                hit = jnp.where(key == at, jnp.bfloat16(1), jnp.bfloat16(0))
                (heads if 16 * j < head else tails).append(hit)
        product = lax.dot_general(
            payload[:, span], jnp.concatenate(heads + tails, axis=0), NT, preferred_element_type=jnp.float32
        )
        moved = product if moved is None else moved + product
    first = 0
    for out in outs:
        size = out.shape[1]
        part = moved[first : first + size]
        if first == 0:
            part = jnp.where(over, POISON, part)
        part = part.astype(jnp.bfloat16)
        for d in range(pair):
            out[d, :, : local * head] = part[:, d * local * head : (d + 1) * local * head]
            if tail:
                at = pair * local * head + d * local * tail
                out[d, :, local * head :] = part[:, at : at + local * tail]
        first += size


def permute(covariates, pseudo, honest, destination, node_slot, capacity, local, devices, sizes):
    features, rows = covariates.shape
    nodes = node_slot.shape[0]
    width = local * capacity
    pair = 2 if devices % 2 == 0 else 1
    whole = lambda d: (0, 0)
    return pl.pallas_call(
        functools.partial(permute_kernel, capacity, local, pair),
        grid=(devices // pair,),
        in_specs=[
            pl.BlockSpec((features, rows), whole),
            pl.BlockSpec((16, rows), whole),
            pl.BlockSpec((1, rows), whole),
            pl.BlockSpec((1, rows), whole),
            pl.BlockSpec((1, nodes), whole),
        ],
        out_specs=[pl.BlockSpec((pair, size, width), lambda d: (d, 0, 0)) for size in sizes],
        out_shape=[jax.ShapeDtypeStruct((devices, size, width), jnp.bfloat16) for size in sizes],
        scratch_shapes=[
            pltpu.VMEM((features + 16, rows), jnp.bfloat16),
            pltpu.VMEM((1, rows), jnp.float32),
            pltpu.VMEM((1, rows), jnp.float32),
            pltpu.VMEM((nodes, LANES), jnp.float32),
        ],
        compiler_params=pltpu.CompilerParams(vmem_limit_bytes=VMEM),
    )(covariates, pseudo, honest.reshape(1, rows), destination.reshape(1, rows), node_slot.reshape(1, nodes))


def gather_rows(arrived, first, size, node, capacity, local, store):
    devices = arrived.shape[0]
    head = capacity // LANES * LANES
    tail = capacity - head
    span = slice(first, first + size)
    for s in range(devices):
        store(s * head, arrived[s, span, node * head : (node + 1) * head].astype(jnp.float32))
    if tail:
        each = LANES // tail
        lane = lax.broadcasted_iota(jnp.int32, (size, local * tail), 1)
        for i in range(devices // each):
            columns = []
            for j in range(each):
                block = arrived[each * i + j, span, local * head : local * capacity].astype(jnp.float32)
                columns.append(block[:, node * tail : (node + 1) * tail])
            store(devices * head + i * LANES, jnp.concatenate(columns, axis=1))


def histogram_kernel(capacity, local, first, size, chained, *refs):
    if chained:
        arrived, stats, _, before_ref, out_ref, best_ref, high, low, values = refs
    else:
        arrived, out_ref, best_ref, high, low, values = refs
        stats = arrived
    group = pl.program_id(0)
    rows = high.shape[2]

    @pl.when(group == 0)
    def _():
        if chained:
            best_ref[...] = before_ref[...]
        else:
            best_ref[...] = jnp.full(best_ref.shape, -jnp.inf, jnp.float32)
        for n in range(local):

            def store(at, part):
                level = part - 1.0
                upper = jnp.floor(level * (1.0 / LO))
                span = slice(at, at + part.shape[1])
                high[n, :, span] = upper
                low[n, :, span] = level - upper * LO

            def store_values(at, part):
                values[n, :, at : at + part.shape[1]] = part.astype(jnp.bfloat16)

            gather_rows(arrived, first, size, n, capacity, local, store)
            gather_rows(stats, 0, 16, n, capacity, local, store_values)

    upper = triangle()
    step = math.gcd(rows, 512)
    sub = lax.broadcasted_iota(jnp.int32, (16, step), 0)
    subf = sub.astype(jnp.float32)
    wanted = (sub % 4).astype(jnp.float32)
    zero, one = jnp.bfloat16(0), jnp.bfloat16(1)
    tables = []
    for turn in range(2 * local):
        q, n = turn // local, turn % local
        sums = None
        for c in range(rows // step):
            span = pl.ds(c * step, step)
            stat = values[n, :, span]
            mixed = None
            left_side, right_side = [], []
            for f in range(4):
                row = pl.ds(group * 8 + q * 4 + f, 1)
                top = jnp.broadcast_to(high[n, row, span], (16, step))
                bottom = jnp.broadcast_to(low[n, row, span], (16, step)).astype(jnp.bfloat16)
                mixed = top if f == 0 else jnp.where(sub >= 4 * f, top, mixed)
                top = top.astype(jnp.bfloat16)
                for h in range(HI):
                    left_side.append(jnp.where(top == jnp.bfloat16(h), stat, zero))
                for j in range(LO // 16):
                    at = (subf + float(16 * j)).astype(jnp.bfloat16)
                    right_side.append(jnp.where(bottom == at, one, zero))
            left_side.append(jnp.where(mixed == wanted, 1.0, 0.0).astype(jnp.bfloat16))
            product = lax.dot_general(
                jnp.concatenate(left_side, axis=0),
                jnp.concatenate(right_side, axis=0),
                NT,
                preferred_element_type=jnp.float32,
            )
            sums = product if sums is None else sums + product
        weights = []
        for f in range(4):
            lanes = slice(f * LO, (f + 1) * LO)
            piece = jnp.concatenate([sums[(f * HI + h) * 16 : (f * HI + h + 1) * 16, lanes] for h in range(HI)], axis=1)
            weight = jnp.concatenate([sums[256 + f * HI + h : 257 + f * HI + h, lanes] for h in range(HI)], axis=1)
            out_ref[n, 0, q * 4 + f : q * 4 + f + 1, :] = weight
            out_ref[n, 1:17, q * 4 + f, :] = piece
            tables.append(piece)
            weights.append(weight)
        tables.append(jnp.concatenate(weights + [jnp.zeros((4, B), jnp.float32)], axis=0))
    table = jnp.concatenate(tables, axis=0)
    one_part = table.astype(jnp.bfloat16)
    table = table - one_part.astype(jnp.float32)
    two_part = table.astype(jnp.bfloat16)
    three_part = (table - two_part.astype(jnp.float32)).astype(jnp.bfloat16)
    left = (
        jnp.dot(three_part, upper, preferred_element_type=jnp.float32)
        + jnp.dot(two_part, upper, preferred_element_type=jnp.float32)
        + jnp.dot(one_part, upper, preferred_element_type=jnp.float32)
    )
    total = left[:, B - 1 : B]
    right = total - left
    for turn in range(2 * local):
        n = turn % local
        for f in range(4):
            span = slice(72 * turn + 16 * f, 72 * turn + 16 * f + 16)
            count = slice(72 * turn + 64 + f, 72 * turn + 65 + f)
            squared = lambda side: jnp.sum(side[span] * side[span], axis=0, keepdims=True) / (side[count] + 1.0)
            gain = squared(left) + squared(right) - squared(total)
            best_ref[n : n + 1, :] = jnp.maximum(best_ref[n : n + 1, :], gain)


def histogram_part(arrived, stats, previous, first, size, offset, features, capacity, local):
    devices, height, width = arrived.shape
    rows = devices * capacity
    groups = size // 8
    whole = lambda g: (0, 0, 0)
    chained = previous is not None
    in_specs = [pl.BlockSpec((devices, height, width), whole)]
    operands = [arrived]
    if chained:
        in_specs += [
            pl.BlockSpec((devices, 16, width), whole),
            pl.BlockSpec(memory_space=pl.ANY),
            pl.BlockSpec((local, B), lambda g: (0, 0)),
        ]
        operands += [stats, previous[0], previous[1]]
    return pl.pallas_call(
        functools.partial(histogram_kernel, capacity, local, first, size, chained),
        grid=(groups,),
        in_specs=in_specs,
        out_specs=[
            pl.BlockSpec((local, 17, 8, B), lambda g: (0, 0, offset // 8 + g, 0)),
            pl.BlockSpec((local, B), lambda g: (0, 0)),
        ],
        out_shape=[
            jax.ShapeDtypeStruct((local, 17, features, B), jnp.float32),
            jax.ShapeDtypeStruct((local, B), jnp.float32),
        ],
        scratch_shapes=[
            pltpu.VMEM((local, size, rows), jnp.float32),
            pltpu.VMEM((local, size, rows), jnp.float32),
            pltpu.VMEM((local, 16, rows), jnp.bfloat16),
        ],
        input_output_aliases={2: 0} if chained else {},
        compiler_params=pltpu.CompilerParams(vmem_limit_bytes=VMEM),
        cost_estimate=pl.CostEstimate(
            flops=4 * local * groups * 272 * 256 * rows, bytes_accessed=arrived.size * 2, transcendentals=0
        ),
    )(*operands)


def swap(block):
    return lax.all_to_all(block, "node", split_axis=0, concat_axis=0, tiled=True)


def finish(first_arrived, sent, features, capacity, local):
    size = first_arrived.shape[1] - 16
    result = histogram_part(first_arrived, None, None, 16, size, 0, features, capacity, local)
    for block in sent:
        arrived = swap(block)
        result = histogram_part(
            arrived, first_arrived, result, 0, block.shape[1], size, features, capacity, local
        )
        size += block.shape[1]
    return tuple(result)


def on_device(covariates, pseudo, honest, destination, node_slot):
    features, rows = covariates.shape
    devices = lax.axis_size("node")
    nodes = node_slot.shape[0]
    local = nodes // devices
    most = 2 * rows // nodes
    early = features // 2
    early = early if early % 16 == 0 else features
    sizes = [16 + early] + ([features - early] if early < features else [])
    small = most - 96 if most % LANES == 0 and most > LANES else most

    def route(capacity):
        return permute(covariates, pseudo, honest, destination, node_slot, capacity, local, devices, sizes)

    def full():
        sent = route(most)
        return finish(swap(sent[0]), sent[1:], features, most, local)

    if small < most:
        sent = route(small)
        arrived = swap(sent[0])
        over = jnp.max(arrived[:, 0, 0]) > POISON / 2
        histogram, best = lax.cond(over, full, lambda: finish(arrived, sent[1:], features, small, local))
    else:
        histogram, best = full()
    best_gain = lax.pmax(jnp.max(best, axis=1), "feat")
    return (jnp.transpose(histogram, (0, 2, 1, 3)), best_gain)


def solution(mesh):
    placed = (P("feat", "node"), P(None, "node"), P("node"), P("node", None), P())
    return jax.shard_map(
        on_device,
        mesh=mesh,
        in_specs=placed,
        out_specs=(P("node", "feat", None, None), P("node")),
        check_vma=False,
    )
```
